128 devices in a mesh: expert: 32 (over z, y, x_hi), replica: 4 (over x_lo, core).
Axes of the slice: x: 4 (x_hi: 2, x_lo: 2; x = x_hi * 2 + x_lo), y: 4, z: 4, core: 2. Of those that a mesh axis runs over, the one named last changes fastest.
Arguments:
- tokens: bfloat16 [16384, 2048], P(('expert', 'replica')), may hold values from -6 to 6
- expert_ids: int32 [16384, 10], P(('expert', 'replica')), may hold values from 0 to 255, all different within a row; in each aligned block of 128 rows (0 to 127, 128 to 255, ...) at most 6 rows name the same one
- router_scores: float32 [16384, 10], P(('expert', 'replica')), may hold values from -8 to 320
- lane_list: int32 [256], replicated, may hold values from 0 to 7, as said below
- capacity: int32 [256], replicated, may hold values from 320 to 640, as said below
- train_gate: bfloat16 [256, 2048, 512], P('expert', 'replica'), may hold values from -0.125 to 0.125
- train_up: bfloat16 [256, 2048, 512], P('expert', 'replica'), may hold values from -0.125 to 0.125
- train_down: bfloat16 [256, 2048, 512], P('expert', 'replica'), may hold values from -0.25 to 0.25
Outputs:
- combined: bfloat16 [16384, 2048], P(('expert', 'replica'))
- rollout_gate: bfloat16 [256, 2048, 512], P(('expert', 'replica'))
- rollout_up: bfloat16 [256, 2048, 512], P(('expert', 'replica'))
- rollout_down: bfloat16 [256, 2048, 512], P(('expert', 'replica'))
The draws below stay inside these ranges and needn't reach their ends.
Inputs may be any that keep to these rules, and one draw needn't show every extreme that they name: `expert_ids`: among the 128 tokens of one device no expert is named by more than 6 tokens, and some device names some expert exactly 6 times. `lane_list`: each run of 8 entries that starts at a multiple of 8 holds each of 0 to 7 once. Some expert has capacity exactly 640.
All inputs are finite; a program needn't handle non-finite values.
Results may differ from the reference program's by a relative error of at most 0.0058.
Values may be sent and summed in bfloat16 or wider, within the bound.
A program may use at most 128 MiB of HBM per device.

```python
import math
import jax
import jax.numpy as jnp
import numpy as np
from jax import lax

D = 2048
H = 512
TOP = 10
EXP_DEV = 2
TOK_DEV = 128
LANES = 8
EXPERTS = 256
TOKENS = 16384
CAP_SRC = 6
MEAN_LOAD = 640
N_EXPERT = 32
N_REPLICA = 4


def draw_lane_list(key, part):
    key = jax.random.fold_in(key, 11)
    group_keys = jax.random.split(key, EXPERTS // LANES)
    orders = jax.vmap(lambda member_key: jax.random.permutation(member_key, LANES))(group_keys)
    return orders.reshape(-1).astype(jnp.int32)


def draw_capacity(key, part):
    key = jax.random.fold_in(key, 23)
    value_key, spot_key = jax.random.split(key)
    values = jax.random.randint(value_key, (EXPERTS,), MEAN_LOAD // 2, MEAN_LOAD + 1)
    spot = jax.random.randint(spot_key, (), 0, EXPERTS)
    filled = jnp.where(jnp.arange(EXPERTS) == spot, MEAN_LOAD, values)
    return filled.astype(jnp.int32)


def draw_router_scores(key, part):
    key = jax.random.fold_in(key, 37)
    score_keys = jax.random.split(key, 1)
    scores = jnp.clip(1.5 * jax.random.normal(score_keys[0], (TOKENS, TOP), jnp.float32), -8.0, 8.0)
    return scores.astype(jnp.float32)


def block_levels(key, shape, cuts, smallest, high):
    def one(axis_at, blocks):
        draws = jax.random.uniform(jax.random.fold_in(jax.random.fold_in(key, 6), axis_at), (blocks,), jnp.float32, smallest / len(cuts), high / len(cuts))
        return jnp.repeat(jnp.exp(draws), shape[axis_at] // blocks).reshape((-1,) + (1,) * (len(shape) - axis_at - 1))

    loudness = one(*cuts[0])
    for cut in cuts[1:]:
        loudness = loudness * one(*cut)
    return loudness


def assign_block(rng, own, number, rows, number_of, top, limit, lean):
    order = jax.random.permutation(rng, number_of)
    crowded, usual = shares(number_of, rows * top, limit, lean, True), shares(number_of, rows * top, limit, lean, False)
    places = jnp.arange(number_of)

    def named(lengths, turn):
        used = int((lengths > 0).sum())
        fixed = max(1, used // 4)
        moved = fixed + (places - fixed + turn * (used - fixed)) % max(1, number_of - fixed)
        return jnp.zeros((number_of,), jnp.int32).at[order[jnp.where(places < fixed, places, moved)]].set(jnp.asarray(lengths, jnp.int32))

    lengths = jnp.where(number % 4 == 0, named(crowded, number // 4), named(usual, number - number // 4 - 1))
    mixed = jax.random.permutation(jax.random.fold_in(own, 3), number_of)
    giver, sink = mixed[0:number_of // 2 * 2:2], mixed[1:number_of // 2 * 2:2]
    slack = jnp.minimum(lengths[giver] - 1, limit - lengths[sink]) // 2
    slack = jnp.where((giver == order[0]) | (sink == order[0]) | (lengths[sink] == 0), 0, jnp.maximum(slack, 0))
    moved = jax.random.randint(jax.random.fold_in(own, 4), (number_of // 2,), 0, 1 << 20) % (slack + 1)
    lengths = lengths.at[giver].add(-moved).at[sink].add(moved)
    items = jnp.searchsorted(jnp.cumsum(lengths), jnp.arange(rows * top), side="right").astype(jnp.int32)
    table = items.reshape(top, rows).T
    table = table[jax.random.permutation(jax.random.fold_in(own, 1), rows)]
    turn = jax.random.randint(jax.random.fold_in(own, 2), (rows, 1), 0, top)
    return jnp.take_along_axis(table, (jnp.arange(top)[None, :] + turn) % top, axis=1)


def shares(number_of, total, bound, skew, full):
    weights = [(1 << 20) // math.isqrt(grade ** skew) + 1 for grade in range(1, number_of + 1)]
    largest = bound if full else min(bound, max(-(-total // number_of), total * weights[0] // sum(weights)))
    least = 1 if total - largest >= number_of - 1 else 0
    counts, surplus = [largest] + [least] * (number_of - 1), total - largest - least * (number_of - 1)
    while surplus > 0:
        free = [i for i in range(1, number_of) if counts[i] < largest] or [i for i in range(1, number_of) if counts[i] < bound]
        pool, left = sum([weights[i] for i in free]), surplus
        for i in free:
            more = min(bound - counts[i], max(1, left * weights[i] // pool), surplus)
            counts[i] = counts[i] + more
            surplus = surplus - more
    return np.array(counts)


def scatter_about(rng, shape, scale, bound, pieces=(), held_as=jnp.bfloat16):
    gain = block_levels(rng, shape, pieces, -0.22, 0.18) if pieces else 1.0
    result = jax.random.normal(rng, shape, jnp.float32) * scale * gain
    return jnp.minimum(jnp.maximum(result, -bound), bound).astype(held_as)


def setup_inputs(seed: int = 0) -> dict:
    seeds = jax.random.split(jax.random.key(seed), 9)
    tokens = scatter_about(seeds[0], (TOKENS, D), 1.0, 6.0, ((0, 128),))
    expert_ids_keys = jax.random.split(jax.random.fold_in(seeds[1], 1), TOKENS // TOK_DEV)
    expert_ids_turns = jax.random.permutation(jax.random.fold_in(seeds[1], 3), TOKENS // TOK_DEV)
    expert_ids = jax.vmap(lambda own, number: assign_block(jax.random.fold_in(seeds[1], 2), own, number, TOK_DEV, EXPERTS, TOP, CAP_SRC, 1))(expert_ids_keys, expert_ids_turns).reshape((TOKENS, TOP))
    router_scores = draw_router_scores(jax.random.fold_in(seeds[8], 71), 0)
    lane_list = draw_lane_list(jax.random.fold_in(seeds[8], 71), 0)
    capacity = draw_capacity(jax.random.fold_in(seeds[8], 71), 0)
    train_gate = scatter_about(seeds[5], (EXPERTS, D, H), D ** -0.5, 0.125, ((0, 32), (1, 4)))
    train_up = scatter_about(seeds[6], (EXPERTS, D, H), D ** -0.5, 0.125, ((0, 32), (1, 4)))
    train_down = scatter_about(seeds[7], (EXPERTS, D, H), H ** -0.5, 0.25, ((0, 32), (1, 4)))
    return dict(tokens=tokens, expert_ids=expert_ids, router_scores=router_scores, lane_list=lane_list, capacity=capacity, train_gate=train_gate, train_up=train_up, train_down=train_down)


def reference(tokens, expert_ids, router_scores, lane_list, capacity, train_gate, train_up, train_down):
    lane_count = EXP_DEV * N_REPLICA
    slots = jnp.arange(EXPERTS, dtype=jnp.int32)
    column = slots // lane_count
    lane_index = slots % lane_count
    grouped = lane_list.reshape(N_EXPERT, lane_count)
    chosen = grouped[column]
    lane_range = jnp.arange(lane_count, dtype=jnp.int32)
    within = jnp.sum(jnp.where(chosen == lane_index[:, None], lane_range[None, :], 0), axis=1)
    source = (column * lane_count + within).astype(jnp.int32)
    rollout_gate = train_gate[source]
    rollout_up = train_up[source]
    rollout_down = train_down[source]
    gates = jax.nn.softmax(router_scores.astype(jnp.float32), axis=-1)
    position = jnp.arange(MEAN_LOAD, dtype=jnp.int32)

    def one_expert(total, expert):
        named = jnp.any(expert_ids == expert, axis=1)
        picked = jnp.nonzero(named, size=MEAN_LOAD, fill_value=0)[0].astype(jnp.int32)
        live = (position < jnp.sum(named.astype(jnp.int32))) & (position < capacity[expert])
        rows = tokens[picked]
        gate_part = jnp.dot(rows, train_gate[expert], preferred_element_type=jnp.float32)
        up_part = jnp.dot(rows, train_up[expert], preferred_element_type=jnp.float32)
        hidden = (jax.nn.silu(gate_part) * up_part).astype(jnp.bfloat16)
        outputs = jnp.dot(hidden, train_down[expert].T, preferred_element_type=jnp.float32).astype(jnp.bfloat16)
        weight = jnp.sum(jnp.where(expert_ids[picked] == expert, gates[picked], 0.0), axis=1)
        weight = jnp.where(live, weight, 0.0)
        return total.at[picked].add(weight[:, None] * outputs.astype(jnp.float32)), None

    total = jnp.zeros(tokens.shape, jnp.float32)
    total, unused = lax.scan(one_expert, total, jnp.arange(EXPERTS, dtype=jnp.int32))
    return total.astype(jnp.bfloat16), rollout_gate, rollout_up, rollout_down
```

```python
import jax
import jax.numpy as jnp
from jax import lax
from jax.experimental import pallas as pl
from jax.experimental.pallas import tpu as pltpu
from jax.sharding import PartitionSpec as P

MESH = pl.DeviceIdType.MESH
BF = jnp.bfloat16
F32 = jnp.float32
ROWS = 48
PEERS = 16
ALL = ROWS * PEERS
D = 2048
H = 512


def kernel(
    tok, ids, scores, lane, cap, tg, tu, td,
    comb, og, ou, od,
    big, stage, wbuf, xall, send, recv, pmat, wmat, hid, idr, bout, binr,
    meta, mask3, key3, gate3, cnt, tmp,
    s_t, s_x, r_x, s_meta, r_meta, s_w, r_w, l_w, s_cnt, r_cnt, s_d, r_d,
    s_ret, r_ret, s_sib, r_sib, s_idle, r_idle, s_busy, r_busy, l_x, l_in,
):
    e = lax.axis_index("expert")
    r = lax.axis_index("replica")
    g, xh = e // 2, e % 2
    xl, c = r // 2, r % 2
    z, y = g // 4, g % 4
    o = xh * 4 + r
    tgt = (r, r + 1 - 2 * c, (r + 2) % 4, 3 - r)
    e_far = e + 1 - 2 * xh
    train, outs = (tg, tu, td), (og, ou, od)

    def dev(ee, rr):
        return {"expert": ee, "replica": rr}

    def plane(dz, dy):
        return dev((((z + dz + 4) % 4) * 4 + (y + dy + 4) % 4) * 2 + xh, r)

    def remote(src, dst, ssem, rsem, device):
        return pltpu.make_async_remote_copy(
            src_ref=src, dst_ref=dst, send_sem=ssem, recv_sem=rsem, device_id=device, device_id_type=MESH
        )

    def wait(ref, sem):
        pltpu.make_async_copy(ref, ref, sem).wait()

    loads = [pltpu.make_async_copy(train[w], big.at[pl.ds(w * 4096, 4096)], s_t.at[w]) for w in range(3)]
    for copy in loads:
        copy.start()
    tmp[...] = jnp.full((128, 128), -1.0, F32)
    tmp[:, 0:10] = ids[...].astype(F32)
    meta[o, 0:16, :] = jnp.transpose(tmp[...])[0:16]
    raw = scores[...]
    grown = jnp.exp(raw - jnp.max(raw, axis=1, keepdims=True))
    tmp[:, 0:10] = grown / jnp.sum(grown, axis=1, keepdims=True)
    meta[o, 16:32, :] = jnp.transpose(tmp[...])[0:16]

    barrier = pltpu.get_barrier_semaphore()
    group = [dev(e if f < 4 else e_far, tgt[f % 4]) for f in range(1, 8)]
    for device in group:
        pl.semaphore_signal(barrier, inc=1, device_id=device, device_id_type=MESH)

    def greet(m, _):
        pl.semaphore_signal(barrier, inc=1, device_id=plane(m // 4, m % 4), device_id_type=MESH)
        return 0

    lax.fori_loop(1, PEERS, greet, 0)
    pl.semaphore_wait(barrier, 7 + PEERS - 1)

    def block(b):
        return xall.at[pl.ds(pl.multiple_of(b * 128, 128), 128)]

    sib, busy, idle = dev(e, tgt[1]), dev(e, tgt[2]), dev(e_far, tgt[2])
    x_sends = [
        remote(tok, block(o), s_x.at[0], r_x.at[o], busy),
        remote(tok, block(o), s_x.at[1], r_x.at[o], idle),
        remote(tok, block(o), s_x.at[2], r_x.at[o], sib),
    ]
    for copy in x_sends:
        copy.start()
    own_x = pltpu.make_async_copy(tok, block(o), l_x)
    own_x.start()
    for device in group:
        remote(meta.at[o], meta.at[o], s_meta, r_meta, device).start()

    def find(column, k, table=None):
        at = jnp.int32(0)
        for j in range(8):
            at = at + jnp.where(lane[column * 8 + j] == k, j if table is None else table[column * 8 + j], 0)
        return at

    lanes = [lane[e * 8 + j] for j in range(8)]
    own_w = {}
    for i in range(2):
        for w in range(3):
            if i == 0:
                loads[w].wait()
            for k in (2, 3, 1, 0):
                n = (i * 3 + w) * 4 + k

                def choose(t, _):
                    at = pl.multiple_of(t * 64, 64)
                    kept = big[pl.ds(pl.multiple_of(w * 4096 + at, 64), 64), :]
                    for j in range(1, 8):
                        other = big[pl.ds(pl.multiple_of((w * 8 + j) * 512 + at, 64), 64), :]
                        kept = lax.select(lanes[j] == 2 * tgt[k] + i, other, kept)
                    stage[n, pl.ds(at, 64), :] = kept
                    return 0

                lax.fori_loop(0, 8, choose, 0)
                place = outs[w].at[i, pl.ds(pl.multiple_of(r * 512, 512), 512)]
                if k:
                    remote(stage.at[n], place, s_w, r_w.at[i, w, k], dev(e, tgt[k])).start()
                else:
                    own_w[i, w] = pltpu.make_async_copy(stage.at[n], place, l_w.at[i, w])
                    own_w[i, w].start()

    wait(meta.at[0:7], r_meta)
    named = [meta[:, k, :] for k in range(10)]
    gates = [meta[:, 16 + k, :] for k in range(10)]

    def expert_of(s):
        column = (s // 2) * 2 + xh
        return column * 8 + find(column, 2 * r + s % 2)

    def one_slot(s, _):
        expert = expert_of(s).astype(F32)
        hits = jnp.zeros((8, 128), F32)
        gate = jnp.zeros((8, 128), F32)
        for k in range(10):
            same = named[k] == expert
            hits = hits + jnp.where(same, 1.0, 0.0)
            gate = gate + jnp.where(same, gates[k], 0.0)
        mask3[s] = hits
        gate3[s] = gate
        return 0

    lax.fori_loop(0, 32, one_slot, 0)
    hits = mask3[...].reshape(256, 128)
    hits16 = hits.astype(BF)
    row = lax.broadcasted_iota(jnp.int32, (256, 256), 0)
    col = lax.broadcasted_iota(jnp.int32, (256, 256), 1)
    slot_same = (row >> 3) == (col >> 3)
    earlier_block = jnp.where(slot_same & (col < row), 1.0, 0.0).astype(BF)
    any_block = jnp.where(slot_same, 1.0, 0.0).astype(BF)
    earlier_token = jnp.where(row[0:128, 0:128] < col[0:128, 0:128], 1.0, 0.0).astype(BF)
    ones = jnp.ones((128, 128), BF)

    def mm(a, b):
        return jnp.dot(a, b, preferred_element_type=F32)

    rank = mm(hits16, earlier_token) + mm(mm(earlier_block, hits16).astype(BF), ones)
    key3[...] = jnp.where(hits > 0.5, rank, -1.0).reshape(32, 8, 128)
    mask3[...] = mm(mm(any_block, hits16).astype(BF), ones).reshape(32, 8, 128)
    cnt[g] = mask3[:, 0, :]

    def tell(m, _):
        remote(cnt.at[g], cnt.at[g], s_cnt, r_cnt, plane(m // 4, m % 4)).start()
        return 0

    lax.fori_loop(1, PEERS, tell, 0)

    ob, oi, oa = xh * 4 + tgt[2], (1 - xh) * 4 + tgt[2], (1 - xh) * 4 + r
    wait(block(ob), r_x.at[ob])
    x_sends.append(remote(block(ob), block(ob), s_x.at[3], r_x.at[ob], idle))
    x_sends.append(remote(block(ob), block(ob), s_x.at[4], r_x.at[ob], sib))
    x_sends[3].start()
    x_sends[4].start()
    wait(block(oi), r_x.at[oi])
    x_sends.append(remote(block(oi), block(oi), s_x.at[5], r_x.at[oi], sib))
    x_sends[5].start()
    wait(block(oa), r_x.at[oa])
    x_sends.append(remote(block(oa), block(oa), s_x.at[6], r_x.at[oa], sib))
    x_sends[6].start()
    own_x.wait()
    for b in (xh * 4 + tgt[1], xh * 4 + tgt[3], (1 - xh) * 4 + tgt[1], (1 - xh) * 4 + tgt[3]):
        wait(block(b), r_x.at[b])

    place48 = lax.broadcasted_iota(jnp.int32, (ROWS, 128), 0).astype(F32)

    def slot_at(m, i):
        dz, dy = m // 4, m % 4
        return (((z + dz) % 4) * 4 + (y + dy) % 4) * 2 + i

    place16 = place48[0:16]
    for i in range(2):
        for p in range(3):
            piece = i * 3 + p

            def pick(m, _):
                at = key3[slot_at(m, i)] - 16.0 * p
                for b in range(8):
                    pmat[pl.ds(pl.multiple_of(m * 16, 16), 16), b * 128 : b * 128 + 128] = jnp.where(
                        at[b : b + 1, :] == place16, 1.0, 0.0
                    ).astype(BF)
                return 0

            lax.fori_loop(0, PEERS, pick, 0)

            def gather(n, _):
                cols = pl.ds(pl.multiple_of(n * 512, 512), 512)
                send[piece, :, cols] = mm(pmat[0:256, :], xall[:, cols]).astype(BF)
                return 0

            lax.fori_loop(0, 4, gather, 0)

            def dispatch(m, _):
                src = send.at[piece, pl.ds(pl.multiple_of(m * 16, 16), 16)]
                dst = recv.at[i, pl.ds(pl.multiple_of(m * ROWS + p * 16, 16), 16)]
                remote(src, dst, s_d, r_d.at[i], plane(m // 4, m % 4)).start()
                return 0

            lax.fori_loop(1, PEERS, dispatch, 0)
            recv[i, p * 16 : p * 16 + 16, :] = send[piece, 0:16, :]

    wait(cnt.at[0:15], r_cnt)

    def before(p, total):
        return total + cnt[p] * jnp.where(p < g, 1.0, 0.0)

    seen = lax.fori_loop(0, PEERS, before, jnp.zeros((32, 128), F32))
    tmp[0:32, :] = seen

    def drop(s, _):
        room = find((s // 2) * 2 + xh, 2 * r + s % 2, cap).astype(F32) - tmp[pl.ds(s, 1), :]
        gate3[s] = jnp.where(key3[s] < room, gate3[s], 0.0)
        return 0

    lax.fori_loop(0, 32, drop, 0)

    def weigh(i, half):
        def fill(n, _):
            s = slot_at(half * 8 + n, i)
            at, gate = key3[s], gate3[s]
            for b in range(8):
                spot = (b % 2) * 4 + b // 2
                pmat[pl.ds(pl.multiple_of(n * ROWS, 16), ROWS), spot * 128 : spot * 128 + 128] = jnp.where(
                    at[b : b + 1, :] == place48, gate[b : b + 1, :], 0.0
                ).astype(BF)
            return 0

        lax.fori_loop(0, 8, fill, 0)
        wmat[i, :, half * 384 : half * 384 + 384] = jnp.transpose(pmat[...])

    for i in range(2):
        for half in range(2):
            weigh(i, half)

    def block_of(i, w, k):
        return outs[w].at[i, pl.ds(pl.multiple_of(tgt[k] * 512, 512), 512)]

    def arrived(i, w, k):
        if k:
            wait(block_of(i, w, k), r_w.at[i, w, k])
        else:
            own_w[i, w].wait()

    def hidden(i):
        wait(recv.at[i, 0:720], r_d.at[i])
        fetch = []
        for w in range(2):
            for k in range(4):
                arrived(i, w, k)
            fetch.append(pltpu.make_async_copy(outs[w].at[i], wbuf.at[w], l_in.at[w]))
            fetch[w].start()
        for copy in fetch:
            copy.wait()

        def part(n, _):
            cols = pl.ds(pl.multiple_of(n * 256, 256), 256)
            gate = mm(recv[i], wbuf[0, :, cols])
            up = mm(recv[i], wbuf[1, :, cols])
            hid[:, cols] = (gate / (1.0 + jnp.exp(-gate)) * up).astype(BF)
            return 0

        lax.fori_loop(0, 2, part, 0)

    def returned(i, k):
        return big.at[pl.ds((i * 4 + k) * ALL, ALL)]

    def produce(i, k):
        arrived(i, 2, k)
        here = wbuf.at[2, pl.ds(k * 512, 512)]
        fetch = pltpu.make_async_copy(block_of(i, 2, k), here, l_in.at[2])
        fetch.start()
        fetch.wait()
        for n in range(2):
            at = k * 512 + n * 256
            recv[i, :, at : at + 256] = lax.dot_general(
                hid[...], wbuf[2, at : at + 256, :], (((1,), (1,)), ((), ())), preferred_element_type=F32
            ).astype(BF)

        def give_back(m, _):
            src = recv.at[i, pl.ds(pl.multiple_of(m * ROWS, 16), ROWS), pl.ds(k * 512, 512)]
            dst = big.at[pl.ds(pl.multiple_of((i * 4 + k) * ALL + m * ROWS, 16), ROWS)]
            remote(src, dst, s_ret, r_ret.at[i, k], plane(-(m // 4), -(m % 4))).start()
            return 0

        lax.fori_loop(1, PEERS, give_back, 0)
        big[(i * 4 + k) * ALL : (i * 4 + k) * ALL + ROWS, :] = recv[i, 0:ROWS, k * 512 : k * 512 + 512]

    def partial(k):
        return 6144 + k * 1024

    def sibling(k):
        return 10240 + k * 512

    tail = []

    def combine(k):
        for i in range(2):
            base = (i * 4 + k) * ALL
            wait(big.at[pl.ds(base, 720)], r_ret.at[i, k])
        for n in range(2):
            cols = slice(n * 256, n * 256 + 256)
            total = mm(wmat[0], big[k * ALL : k * ALL + ALL, cols])
            total = total + mm(wmat[1], big[(4 + k) * ALL : (4 + k) * ALL + ALL, cols])
            big[partial(k) : partial(k) + 1024, cols] = total.astype(BF)
        k2 = k ^ 1
        tail.append(
            remote(
                big.at[pl.ds(pl.multiple_of(partial(k) + (1 - c) * 512, 512), 512)],
                big.at[pl.ds(sibling(k2), 512)],
                s_sib.at[k], r_sib.at[k2], sib,
            )
        )
        tail[-1].start()

    def own(k):
        return pl.multiple_of(partial(k) + c * 512, 512)

    def to_idle(k):
        wait(big.at[pl.ds(sibling(k), 512)], r_sib.at[k])
        both = big[pl.ds(own(k), 512), :].astype(F32) + big[sibling(k) : sibling(k) + 512, :].astype(F32)
        big[pl.ds(own(k), 512), :] = both.astype(BF)
        k2 = k ^ 2
        tail.append(
            remote(
                big.at[pl.ds(pl.multiple_of(own(k) + (1 - xh) * 256, 256), 256)],
                idr.at[k2], s_idle.at[k], r_idle.at[k2], idle,
            )
        )
        tail[-1].start()

    def to_busy(k):
        wait(idr.at[k], r_idle.at[k])
        there = pl.multiple_of((1 - xl) * 128, 128)
        mine = big[pl.ds(pl.multiple_of(own(k) + xh * 256 + (1 - xl) * 128, 128), 128), :].astype(F32)
        bout[k] = (mine + idr[k, pl.ds(there, 128), :].astype(F32)).astype(BF)
        k2 = k ^ 2
        tail.append(remote(bout.at[k], binr.at[k2], s_busy.at[k], r_busy.at[k2], busy))
        tail[-1].start()

    def finish(k):
        wait(binr.at[k], r_busy.at[k])
        here = pl.multiple_of(xl * 128, 128)
        mine = big[pl.ds(pl.multiple_of(own(k) + xh * 256 + xl * 128, 128), 128), :].astype(F32)
        total = mine + idr[k, pl.ds(here, 128), :].astype(F32) + binr[k].astype(F32)
        comb[:, pl.ds(pl.multiple_of(tgt[k] * 512, 512), 512)] = total.astype(BF)

    hidden(0)
    for k in range(4):
        produce(0, k)
    hidden(1)
    produce(1, 0)
    produce(1, 1)
    produce(1, 2)
    combine(0)
    combine(1)
    produce(1, 3)
    to_idle(0)
    to_idle(1)
    combine(2)
    combine(3)
    to_idle(2)
    to_idle(3)
    to_busy(2)
    to_busy(3)
    to_busy(0)
    to_busy(1)
    for k in (2, 3, 0, 1):
        finish(k)

    for copy in x_sends + tail:
        copy.wait_send()
    wait(meta.at[0:7], s_meta)
    wait(stage.at[0:18], s_w)
    wait(cnt.at[0:15], s_cnt)
    wait(recv.at[:, 0:720], s_d)
    wait(recv.at[:, 0:720], s_ret)


def local(tokens, expert_ids, router_scores, lane_list, capacity, train_gate, train_up, train_down):
    dma = pltpu.SemaphoreType.DMA
    out_w = jax.ShapeDtypeStruct((2, D, H), BF)
    anywhere = pl.BlockSpec(memory_space=pl.ANY)
    vmem = pl.BlockSpec(memory_space=pltpu.VMEM)
    smem = pl.BlockSpec(memory_space=pltpu.SMEM)
    return pl.pallas_call(
        kernel,
        out_shape=(jax.ShapeDtypeStruct((128, D), BF), out_w, out_w, out_w),
        in_specs=[anywhere, vmem, vmem, smem, smem, anywhere, anywhere, anywhere],
        out_specs=[vmem, anywhere, anywhere, anywhere],
        scratch_shapes=[
            pltpu.VMEM((12288, 512), BF),
            pltpu.VMEM((24, 512, 512), BF),
            pltpu.VMEM((3, D, H), BF),
            pltpu.VMEM((1024, D), BF),
            pltpu.VMEM((6, 256, D), BF),
            pltpu.VMEM((2, ALL, D), BF),
            pltpu.VMEM((384, 1024), BF),
            pltpu.VMEM((2, 1024, ALL), BF),
            pltpu.VMEM((ALL, H), BF),
            pltpu.VMEM((4, 256, 512), BF),
            pltpu.VMEM((4, 128, 512), BF),
            pltpu.VMEM((4, 128, 512), BF),
            pltpu.VMEM((8, 32, 128), F32),
            pltpu.VMEM((32, 8, 128), F32),
            pltpu.VMEM((32, 8, 128), F32),
            pltpu.VMEM((32, 8, 128), F32),
            pltpu.VMEM((16, 32, 128), F32),
            pltpu.VMEM((128, 128), F32),
            dma((3,)), dma((7,)), dma((8,)), dma, dma, dma, dma((2, 3, 4)), dma((2, 3)), dma, dma,
            dma, dma((2,)), dma, dma((2, 4)),
            dma((4,)), dma((4,)), dma((4,)), dma((4,)), dma((4,)), dma((4,)), dma, dma((3,)),
        ],
        compiler_params=pltpu.CompilerParams(
            collective_id=0, has_side_effects=True, vmem_limit_bytes=63 << 20
        ),
        name="resync_moe",
    )(
        tokens, expert_ids, router_scores, lane_list, capacity,
        train_gate.reshape(4096, 512), train_up.reshape(4096, 512), train_down.reshape(4096, 512),
    )


def solution(mesh):
    both = ("expert", "replica")
    return jax.shard_map(
        local,
        mesh=mesh,
        in_specs=(
            P(both, None), P(both, None), P(both, None), P(), P(),
            P("expert", "replica", None), P("expert", "replica", None), P("expert", "replica", None),
        ),
        out_specs=(P(both, None), P(both, None, None), P(both, None, None), P(both, None, None)),
        check_vma=False,
    )
```

```python
import jax
import jax.numpy as jnp
from jax import lax
from jax.experimental import pallas as pl
from jax.experimental.pallas import tpu as pltpu
from jax.sharding import PartitionSpec as P

MESH = pl.DeviceIdType.MESH
BF = jnp.bfloat16
F32 = jnp.float32
ROWS = 48
PEERS = 16
ALL = ROWS * PEERS
D = 2048
H = 512


def kernel(
    tok, ids, scores, lane, cap, tg, tu, td,
    comb, og, ou, od,
    big, stage, wbuf, xall, send, recv, pmat, wmat, hid, idr, bout, binr,
    meta, mask3, key3, row3, gate3, cnt, tmp,
    s_t, s_x, r_x, s_meta, r_meta, s_w, r_w, s_cnt, r_cnt, s_d, r_d,
    s_ret, r_ret, s_sib, r_sib, s_idle, r_idle, s_busy, r_busy, l_x, l_in,
):
    e = lax.axis_index("expert")
    r = lax.axis_index("replica")
    g, xh = e // 2, e % 2
    xl, c = r // 2, r % 2
    z, y = g // 4, g % 4
    o = xh * 4 + r
    tgt = (r, r + 1 - 2 * c, (r + 2) % 4, 3 - r)
    e_far = e + 1 - 2 * xh
    train, outs = (tg, tu, td), (og, ou, od)

    def dev(ee, rr):
        return {"expert": ee, "replica": rr}

    def plane(dz, dy):
        return dev((((z + dz + 4) % 4) * 4 + (y + dy + 4) % 4) * 2 + xh, r)

    def remote(src, dst, ssem, rsem, device):
        return pltpu.make_async_remote_copy(
            src_ref=src, dst_ref=dst, send_sem=ssem, recv_sem=rsem, device_id=device, device_id_type=MESH
        )

    def wait(ref, sem):
        pltpu.make_async_copy(ref, ref, sem).wait()

    loads = [pltpu.make_async_copy(train[w], big.at[pl.ds(w * 4096, 4096)], s_t.at[w]) for w in range(3)]
    for copy in loads:
        copy.start()
    meta[o, 0:10, :] = ids[...].astype(F32)
    raw = scores[...]
    grown = jnp.exp(raw - jnp.max(raw, axis=0, keepdims=True))
    meta[o, 16:26, :] = grown / jnp.sum(grown, axis=0, keepdims=True)

    barrier = pltpu.get_barrier_semaphore()
    group = [dev(e if f < 4 else e_far, tgt[f % 4]) for f in range(1, 8)]
    for device in group:
        pl.semaphore_signal(barrier, inc=1, device_id=device, device_id_type=MESH)

    def greet(m, _):
        pl.semaphore_signal(barrier, inc=1, device_id=plane(m // 4, m % 4), device_id_type=MESH)
        return 0

    lax.fori_loop(1, PEERS, greet, 0)
    pl.semaphore_wait(barrier, 7 + PEERS - 1)

    def block(b):
        return xall.at[pl.ds(pl.multiple_of(b * 128, 128), 128)]

    sib, busy, idle = dev(e, tgt[1]), dev(e, tgt[2]), dev(e_far, tgt[2])
    x_sends = [
        remote(tok, block(o), s_x.at[0], r_x.at[o], busy),
        remote(tok, block(o), s_x.at[1], r_x.at[o], idle),
        remote(tok, block(o), s_x.at[2], r_x.at[o], sib),
    ]
    for copy in x_sends:
        copy.start()
    own_x = pltpu.make_async_copy(tok, block(o), l_x)
    own_x.start()
    for device in group:
        remote(meta.at[o], meta.at[o], s_meta, r_meta, device).start()

    def find(column, k, table=None):
        at = jnp.int32(0)
        for j in range(8):
            at = at + jnp.where(lane[column * 8 + j] == k, j if table is None else table[column * 8 + j], 0)
        return at

    lanes = [lane[e * 8 + j] for j in range(8)]
    for i in range(2):
        for w in range(3):
            if i == 0:
                loads[w].wait()
            for k in (2, 3, 1, 0):
                n = (i * 3 + w) * 4 + k

                def choose(t, _):
                    at = pl.multiple_of(t * 64, 64)
                    kept = big[pl.ds(pl.multiple_of(w * 4096 + at, 64), 64), :]
                    for j in range(1, 8):
                        other = big[pl.ds(pl.multiple_of((w * 8 + j) * 512 + at, 64), 64), :]
                        kept = lax.select(lanes[j] == 2 * tgt[k] + i, other, kept)
                    stage[n, pl.ds(at, 64), :] = kept
                    return 0

                lax.fori_loop(0, 8, choose, 0)
                place = outs[w].at[i, pl.ds(pl.multiple_of(r * 512, 512), 512)]
                if k:
                    remote(stage.at[n], place, s_w, r_w.at[i, w, r], dev(e, tgt[k])).start()
                else:
                    pltpu.make_async_copy(stage.at[n], place, r_w.at[i, w, r]).start()

    wait(meta.at[0:7], r_meta)
    named = [meta[:, k, :] for k in range(10)]
    gates = [meta[:, 16 + k, :] for k in range(10)]

    def expert_of(s):
        column = (s // 2) * 2 + xh
        return column * 8 + find(column, 2 * r + s % 2)

    def one_slot(s, _):
        expert = expert_of(s).astype(F32)
        hits = jnp.zeros((8, 128), F32)
        gate = jnp.zeros((8, 128), F32)
        for k in range(10):
            same = named[k] == expert
            hits = hits + jnp.where(same, 1.0, 0.0)
            gate = gate + jnp.where(same, gates[k], 0.0)
        mask3[s] = hits
        gate3[s] = gate
        return 0

    lax.fori_loop(0, 32, one_slot, 0)
    hits = mask3[...].reshape(256, 128)
    hits16 = hits.astype(BF)
    row = lax.broadcasted_iota(jnp.int32, (256, 256), 0)
    col = lax.broadcasted_iota(jnp.int32, (256, 256), 1)
    slot_same = (row >> 3) == (col >> 3)
    earlier_block = jnp.where(slot_same & (col < row), 1.0, 0.0).astype(BF)
    earlier_half = jnp.where(((row >> 2) == (col >> 2)) & (col < row), 1.0, 0.0).astype(BF)
    any_block = jnp.where(slot_same, 1.0, 0.0).astype(BF)
    earlier_token = jnp.where(row[0:128, 0:128] < col[0:128, 0:128], 1.0, 0.0).astype(BF)
    ones = jnp.ones((128, 128), BF)

    def mm(a, b):
        return jnp.dot(a, b, preferred_element_type=F32)

    within = mm(hits16, earlier_token)
    rank = within + mm(mm(earlier_block, hits16).astype(BF), ones)
    key3[...] = rank.reshape(32, 8, 128)
    near = ((row[:, 0:128] >> 2) % 2) == xh
    rank = within + mm(mm(earlier_half, hits16).astype(BF), ones)
    at = jnp.where(near, jnp.where(rank < 16.0, rank, rank + 16.0), jnp.where(rank < 16.0, rank + 16.0, rank + 24.0))
    row3[...] = jnp.where(hits > 0.5, at, -1.0).reshape(32, 8, 128)
    mask3[...] = mm(mm(any_block, hits16).astype(BF), ones).reshape(32, 8, 128)
    cnt[g] = mask3[:, 0, :]

    def tell(m, _):
        remote(cnt.at[g], cnt.at[g], s_cnt, r_cnt, plane(m // 4, m % 4)).start()
        return 0

    lax.fori_loop(1, PEERS, tell, 0)

    def forward(b, n, device):
        x_sends.append(remote(block(b), block(b), s_x.at[n], r_x.at[b], device))
        x_sends[-1].start()

    ob, oi, oa = xh * 4 + tgt[2], (1 - xh) * 4 + tgt[2], (1 - xh) * 4 + r
    wait(block(ob), r_x.at[ob])
    forward(ob, 3, sib)
    forward(ob, 4, idle)
    wait(block(oi), r_x.at[oi])
    forward(oi, 5, sib)

    place48 = lax.broadcasted_iota(jnp.int32, (ROWS, 128), 0).astype(F32)
    place16 = place48[0:16]
    upper = place16 < 8.0
    place8 = jnp.where(upper, place16, place16 - 8.0)

    def slot_at(m, i):
        dz, dy = m // 4, m % 4
        return (((z + dz) % 4) * 4 + (y + dy) % 4) * 2 + i

    def dispatch(late, part):
        half = (1 - xh) if late else xh
        piece = late * 3 + part

        def pick(m, _):
            for b in range(4):
                here = pl.ds(half * 4 + b, 1)
                if part < 2:
                    chosen = row3[slot_at(m, part), here, :] == place16 + 16.0 * late
                else:
                    both = jnp.where(upper, row3[slot_at(m, 0), here, :], row3[slot_at(m, 1), here, :])
                    chosen = both == place8 + (32.0 + 8.0 * late)
                pmat[pl.ds(pl.multiple_of(m * 16, 16), 16), b * 128 : b * 128 + 128] = jnp.where(chosen, 1.0, 0.0).astype(BF)
            return 0

        lax.fori_loop(0, PEERS, pick, 0)

        def gather(n, _):
            cols = pl.ds(pl.multiple_of(n * 512, 512), 512)
            rows = pl.ds(pl.multiple_of(half * 512, 512), 512)
            send[piece, :, cols] = mm(pmat[0:256, 0:512], xall[rows, cols]).astype(BF)
            return 0

        lax.fori_loop(0, 4, gather, 0)
        slot, base = (part, late * 16) if part < 2 else (late, 32)

        def give(m, _):
            src = send.at[piece, pl.ds(pl.multiple_of(m * 16, 16), 16)]
            dst = recv.at[slot, pl.ds(pl.multiple_of(m * ROWS + base, 16), 16)]
            remote(src, dst, s_d, r_d.at[part % 2], plane(m // 4, m % 4)).start()
            return 0

        lax.fori_loop(1, PEERS, give, 0)
        recv[slot, base : base + 16, :] = send[piece, 0:16, :]

    own_x.wait()
    for b in (xh * 4 + tgt[1], xh * 4 + tgt[3]):
        wait(block(b), r_x.at[b])
    for part in (0, 2, 1):
        dispatch(0, part)
    wait(block(oa), r_x.at[oa])
    forward(oa, 6, sib)
    for b in ((1 - xh) * 4 + tgt[1], (1 - xh) * 4 + tgt[3]):
        wait(block(b), r_x.at[b])
    for part in (0, 2, 1):
        dispatch(1, part)

    wait(cnt.at[0:15], r_cnt)

    def before(p, total):
        return total + cnt[p] * jnp.where(p < g, 1.0, 0.0)

    seen = lax.fori_loop(0, PEERS, before, jnp.zeros((32, 128), F32))
    tmp[0:32, :] = seen

    def drop(s, _):
        room = find((s // 2) * 2 + xh, 2 * r + s % 2, cap).astype(F32) - tmp[pl.ds(s, 1), :]
        gate3[s] = jnp.where(key3[s] < room, gate3[s], 0.0)
        return 0

    lax.fori_loop(0, 32, drop, 0)

    def weigh(i, half):
        def fill(n, _):
            s = slot_at(half * 8 + n, i)
            at, gate = row3[s], gate3[s]
            for b in range(8):
                spot = (b % 2) * 4 + b // 2
                pmat[pl.ds(pl.multiple_of(n * ROWS, 16), ROWS), spot * 128 : spot * 128 + 128] = jnp.where(
                    at[b : b + 1, :] == place48, gate[b : b + 1, :], 0.0
                ).astype(BF)
            return 0

        lax.fori_loop(0, 8, fill, 0)
        wmat[i, :, half * 384 : half * 384 + 384] = jnp.transpose(pmat[...])

    for i in range(2):
        for half in range(2):
            weigh(i, half)

    width = (xl * 2, xl * 2 + 1, (1 - xl) * 2, (1 - xl) * 2 + 1)

    def block_of(i, w, k):
        return outs[w].at[i, pl.ds(pl.multiple_of(width[k] * 512, 512), 512)]

    def arrived(i, w, k):
        wait(block_of(i, w, k), r_w.at[i, w, width[k]])

    def hidden(i):
        if i == 0:
            wait(recv.at[:, 0:480], r_d.at[0])

            def sort(m, _):
                rows = pl.ds(pl.multiple_of(m * ROWS + 32, 16), 16)
                near, far = recv[0, rows, :].astype(F32), recv[1, rows, :].astype(F32)
                recv[0, rows, :] = jnp.concatenate([near[0:8], far[0:8]], axis=0).astype(BF)
                recv[1, rows, :] = jnp.concatenate([near[8:16], far[8:16]], axis=0).astype(BF)
                return 0

            lax.fori_loop(0, PEERS, sort, 0)
        else:
            wait(recv.at[0, 0:480], r_d.at[1])
        fetch = []
        for w in range(2):
            for k in range(4):
                arrived(i, w, k)
            fetch.append(pltpu.make_async_copy(outs[w].at[i], wbuf.at[w], l_in.at[w]))
            fetch[w].start()
        for copy in fetch:
            copy.wait()

        def part(n, _):
            cols = pl.ds(pl.multiple_of(n * 256, 256), 256)
            gate = mm(recv[i], wbuf[0, :, cols])
            up = mm(recv[i], wbuf[1, :, cols])
            hid[:, cols] = (gate / (1.0 + jnp.exp(-gate)) * up).astype(BF)
            return 0

        lax.fori_loop(0, 2, part, 0)

    def returned(i, k):
        return big.at[pl.ds((i * 4 + k) * ALL, ALL)]

    def produce(i, k):
        arrived(i, 2, k)
        here = wbuf.at[2, pl.ds(k * 512, 512)]
        fetch = pltpu.make_async_copy(block_of(i, 2, k), here, l_in.at[2])
        fetch.start()
        fetch.wait()
        for n in range(2):
            at = k * 512 + n * 256
            recv[i, :, at : at + 256] = lax.dot_general(
                hid[...], wbuf[2, at : at + 256, :], (((1,), (1,)), ((), ())), preferred_element_type=F32
            ).astype(BF)

        def give_back(m, _):
            src = recv.at[i, pl.ds(pl.multiple_of(m * ROWS, 16), ROWS), pl.ds(k * 512, 512)]
            dst = big.at[pl.ds(pl.multiple_of((i * 4 + k) * ALL + m * ROWS, 16), ROWS)]
            remote(src, dst, s_ret, r_ret.at[i, k], plane(-(m // 4), -(m % 4))).start()
            return 0

        lax.fori_loop(1, PEERS, give_back, 0)
        big[(i * 4 + k) * ALL : (i * 4 + k) * ALL + ROWS, :] = recv[i, 0:ROWS, k * 512 : k * 512 + 512]

    def partial(k):
        return 6144 + k * 1024

    def sibling(k):
        return 10240 + k * 512

    tail = []

    def combine(k):
        for i in range(2):
            base = (i * 4 + k) * ALL
            wait(big.at[pl.ds(base, 720)], r_ret.at[i, k])
        for n in range(2):
            cols = slice(n * 256, n * 256 + 256)
            total = mm(wmat[0], big[k * ALL : k * ALL + ALL, cols])
            total = total + mm(wmat[1], big[(4 + k) * ALL : (4 + k) * ALL + ALL, cols])
            big[partial(k) : partial(k) + 1024, cols] = total.astype(BF)
        k2 = k
        tail.append(
            remote(
                big.at[pl.ds(pl.multiple_of(partial(k) + (1 - c) * 512, 512), 512)],
                big.at[pl.ds(sibling(k2), 512)],
                s_sib.at[k], r_sib.at[k2], sib,
            )
        )
        tail[-1].start()

    def own(k):
        return pl.multiple_of(partial(k) + c * 512, 512)

    def to_idle(k):
        wait(big.at[pl.ds(sibling(k), 512)], r_sib.at[k])
        both = big[pl.ds(own(k), 512), :].astype(F32) + big[sibling(k) : sibling(k) + 512, :].astype(F32)
        big[pl.ds(own(k), 512), :] = both.astype(BF)
        k2 = k ^ 2
        tail.append(
            remote(
                big.at[pl.ds(pl.multiple_of(own(k) + (1 - xh) * 256, 256), 256)],
                idr.at[k2], s_idle.at[k], r_idle.at[k2], idle,
            )
        )
        tail[-1].start()

    def to_busy(k):
        wait(idr.at[k], r_idle.at[k])
        there = pl.multiple_of((1 - xl) * 128, 128)
        mine = big[pl.ds(pl.multiple_of(own(k) + xh * 256 + (1 - xl) * 128, 128), 128), :].astype(F32)
        bout[k] = (mine + idr[k, pl.ds(there, 128), :].astype(F32)).astype(BF)
        k2 = k ^ 2
        tail.append(remote(bout.at[k], binr.at[k2], s_busy.at[k], r_busy.at[k2], busy))
        tail[-1].start()

    def finish(k):
        wait(binr.at[k], r_busy.at[k])
        here = pl.multiple_of(xl * 128, 128)
        mine = big[pl.ds(pl.multiple_of(own(k) + xh * 256 + xl * 128, 128), 128), :].astype(F32)
        total = mine + idr[k, pl.ds(here, 128), :].astype(F32) + binr[k].astype(F32)
        comb[:, pl.ds(pl.multiple_of(width[k] * 512, 512), 512)] = total.astype(BF)

    hidden(0)
    for k in range(4):
        produce(0, k)
    hidden(1)
    for k in range(4):
        produce(1, k)
    combine(0)
    combine(1)
    to_idle(0)
    to_idle(1)
    combine(2)
    to_idle(2)
    to_busy(2)
    combine(3)
    to_idle(3)
    to_busy(3)
    to_busy(0)
    to_busy(1)
    for k in range(4):
        finish(k)

    for copy in x_sends + tail:
        copy.wait_send()
    wait(meta.at[0:7], s_meta)
    wait(stage.at[0:18], s_w)
    wait(cnt.at[0:15], s_cnt)
    wait(recv.at[:, 0:720], s_d)
    wait(recv.at[:, 0:720], s_ret)


def local(tokens, expert_ids, router_scores, lane_list, capacity, train_gate, train_up, train_down):
    dma = pltpu.SemaphoreType.DMA
    out_w = jax.ShapeDtypeStruct((2, D, H), BF)
    anywhere = pl.BlockSpec(memory_space=pl.ANY)
    vmem = pl.BlockSpec(memory_space=pltpu.VMEM)
    smem = pl.BlockSpec(memory_space=pltpu.SMEM)
    return pl.pallas_call(
        kernel,
        out_shape=(jax.ShapeDtypeStruct((128, D), BF), out_w, out_w, out_w),
        in_specs=[anywhere, vmem, vmem, smem, smem, anywhere, anywhere, anywhere],
        out_specs=[vmem, anywhere, anywhere, anywhere],
        scratch_shapes=[
            pltpu.VMEM((12288, 512), BF),
            pltpu.VMEM((24, 512, 512), BF),
            pltpu.VMEM((3, D, H), BF),
            pltpu.VMEM((1024, D), BF),
            pltpu.VMEM((6, 256, D), BF),
            pltpu.VMEM((2, ALL, D), BF),
            pltpu.VMEM((384, 1024), BF),
            pltpu.VMEM((2, 1024, ALL), BF),
            pltpu.VMEM((ALL, H), BF),
            pltpu.VMEM((4, 256, 512), BF),
            pltpu.VMEM((4, 128, 512), BF),
            pltpu.VMEM((4, 128, 512), BF),
            pltpu.VMEM((8, 32, 128), F32),
            pltpu.VMEM((32, 8, 128), F32),
            pltpu.VMEM((32, 8, 128), F32),
            pltpu.VMEM((32, 8, 128), F32),
            pltpu.VMEM((32, 8, 128), F32),
            pltpu.VMEM((16, 32, 128), F32),
            pltpu.VMEM((128, 128), F32),
            dma((3,)), dma((7,)), dma((8,)), dma, dma, dma, dma((2, 3, 4)), dma, dma,
            dma, dma((2,)), dma, dma((2, 4)),
            dma((4,)), dma((4,)), dma((4,)), dma((4,)), dma((4,)), dma((4,)), dma, dma((3,)),
        ],
        compiler_params=pltpu.CompilerParams(
            collective_id=0, has_side_effects=True, vmem_limit_bytes=63 << 20
        ),
        name="resync_moe",
    )(
        tokens, expert_ids.T, router_scores.T, lane_list, capacity,
        train_gate.reshape(4096, 512), train_up.reshape(4096, 512), train_down.reshape(4096, 512),
    )


def solution(mesh):
    both = ("expert", "replica")
    return jax.shard_map(
        local,
        mesh=mesh,
        in_specs=(
            P(both, None), P(both, None), P(both, None), P(), P(),
            P("expert", "replica", None), P("expert", "replica", None), P("expert", "replica", None),
        ),
        out_specs=(P(both, None), P(both, None, None), P(both, None, None), P(both, None, None)),
        check_vma=False,
    )
```

```python
import jax
import jax.numpy as jnp
from jax import lax
from jax.experimental import pallas as pl
from jax.experimental.pallas import tpu as pltpu
from jax.sharding import PartitionSpec as P

MESH = pl.DeviceIdType.MESH
BF = jnp.bfloat16
F32 = jnp.float32
ROWS = 48
PEERS = 16
ALL = ROWS * PEERS
D = 2048
H = 512


def kernel(
    tok, ids, scores, lane, cap, tg, tu, td,
    comb, og, ou, od,
    big, stage, xall, send, recv, pmat, wmat, hid, idr, bout, binr,
    meta, mask3, key3, row3, gate3, cnt, tmp,
    s_t, s_x, r_x, s_meta, r_meta, s_w, r_w, s_cnt, r_cnt, s_d, r_d,
    s_ret, r_ret, s_sib, r_sib, s_idle, r_idle, s_busy, r_busy, l_x,
):
    e = lax.axis_index("expert")
    r = lax.axis_index("replica")
    g, xh = e // 2, e % 2
    xl, c = r // 2, r % 2
    z, y = g // 4, g % 4
    o = xh * 4 + r
    tgt = (r, r + 1 - 2 * c, (r + 2) % 4, 3 - r)
    e_far = e + 1 - 2 * xh
    train, outs = (tg, tu, td), (og, ou, od)

    def dev(ee, rr):
        return {"expert": ee, "replica": rr}

    def plane(dz, dy):
        return dev((((z + dz + 4) % 4) * 4 + (y + dy + 4) % 4) * 2 + xh, r)

    def remote(src, dst, ssem, rsem, device):
        return pltpu.make_async_remote_copy(
            src_ref=src, dst_ref=dst, send_sem=ssem, recv_sem=rsem, device_id=device, device_id_type=MESH
        )

    def wait(ref, sem):
        pltpu.make_async_copy(ref, ref, sem).wait()

    loads = [pltpu.make_async_copy(train[w], big.at[pl.ds(w * 4096, 4096)], s_t.at[w]) for w in range(3)]
    for copy in loads:
        copy.start()
    meta[o, 0:10, :] = ids[...].astype(F32)
    raw = scores[...]
    grown = jnp.exp(raw - jnp.max(raw, axis=0, keepdims=True))
    meta[o, 16:26, :] = grown / jnp.sum(grown, axis=0, keepdims=True)

    lanes = [lane[e * 8 + j] for j in range(8)]
    tgts = (r, r + 1 - 2 * c, (1 - xl) * 2, (1 - xl) * 2 + 1)

    def choose(i, w, k):
        n = (i * 3 + w) * 4 + k

        def some(t, _):
            at = pl.multiple_of(t * 64, 64)
            kept = big[pl.ds(pl.multiple_of(w * 4096 + at, 64), 64), :]
            for j in range(1, 8):
                other = big[pl.ds(pl.multiple_of((w * 8 + j) * 512 + at, 64), 64), :]
                kept = lax.select(lanes[j] == 2 * tgts[k] + i, other, kept)
            stage[n, pl.ds(at, 64), :] = kept
            return 0

        lax.fori_loop(0, 8, some, 0)

    def post(i, w, k):
        n = (i * 3 + w) * 4 + k
        place = outs[w].at[i, pl.ds(pl.multiple_of(r * 512, 512), 512)]
        if k:
            remote(stage.at[n], place, s_w, r_w.at[i, w, r], dev(e, tgts[k])).start()
        else:
            pltpu.make_async_copy(stage.at[n], place, r_w.at[i, w, r]).start()

    def ship(i, w, ks):
        for k in ks:
            choose(i, w, k)
            post(i, w, k)

    barrier = pltpu.get_barrier_semaphore()
    group = [dev(e if f < 4 else e_far, tgt[f % 4]) for f in range(1, 8)]
    for device in group:
        pl.semaphore_signal(barrier, inc=1, device_id=device, device_id_type=MESH)

    def greet(m, _):
        pl.semaphore_signal(barrier, inc=1, device_id=plane(m // 4, m % 4), device_id_type=MESH)
        return 0

    lax.fori_loop(1, PEERS, greet, 0)
    loads[0].wait()
    for k in (2, 3, 1, 0):
        choose(0, 0, k)
    pl.semaphore_wait(barrier, 7 + PEERS - 1)

    def block(b):
        return xall.at[pl.ds(pl.multiple_of(b * 128, 128), 128)]

    sib, busy, idle = dev(e, tgt[1]), dev(e, tgt[2]), dev(e_far, tgt[2])
    x_sends = [
        remote(tok, block(o), s_x.at[0], r_x.at[o], busy),
        remote(tok, block(o), s_x.at[1], r_x.at[o], idle),
        remote(tok, block(o), s_x.at[2], r_x.at[o], sib),
    ]
    for copy in x_sends:
        copy.start()
    own_x = pltpu.make_async_copy(tok, block(o), l_x)
    own_x.start()
    for device in group:
        remote(meta.at[o], meta.at[o], s_meta, r_meta, device).start()
    for k in (2, 3, 1, 0):
        post(0, 0, k)

    wait(meta.at[0:7], r_meta)
    named = [meta[:, k, :] for k in range(10)]
    gates = [meta[:, 16 + k, :] for k in range(10)]

    def find(column, k, table=None):
        at = jnp.int32(0)
        for j in range(8):
            at = at + jnp.where(lane[column * 8 + j] == k, j if table is None else table[column * 8 + j], 0)
        return at

    def expert_of(s):
        column = (s // 2) * 2 + xh
        return column * 8 + find(column, 2 * r + s % 2)

    def one_slot(s, _):
        expert = expert_of(s).astype(F32)
        hits = jnp.zeros((8, 128), F32)
        gate = jnp.zeros((8, 128), F32)
        for k in range(10):
            same = named[k] == expert
            hits = hits + jnp.where(same, 1.0, 0.0)
            gate = gate + jnp.where(same, gates[k], 0.0)
        mask3[s] = hits
        gate3[s] = gate
        return 0

    lax.fori_loop(0, 32, one_slot, 0)
    hits = mask3[...].reshape(256, 128)
    hits16 = hits.astype(BF)
    row = lax.broadcasted_iota(jnp.int32, (256, 256), 0)
    col = lax.broadcasted_iota(jnp.int32, (256, 256), 1)
    slot_same = (row >> 3) == (col >> 3)
    earlier_block = jnp.where(slot_same & (col < row), 1.0, 0.0).astype(BF)
    earlier_half = jnp.where(((row >> 2) == (col >> 2)) & (col < row), 1.0, 0.0).astype(BF)
    any_block = jnp.where(slot_same, 1.0, 0.0).astype(BF)
    earlier_token = jnp.where(row[0:128, 0:128] < col[0:128, 0:128], 1.0, 0.0).astype(BF)
    ones = jnp.ones((128, 128), BF)

    def mm(a, b):
        return jnp.dot(a, b, preferred_element_type=F32)

    within = mm(hits16, earlier_token)
    rank = within + mm(mm(earlier_block, hits16).astype(BF), ones)
    key3[...] = rank.reshape(32, 8, 128)
    near = ((row[:, 0:128] >> 2) % 2) == xh
    rank = within + mm(mm(earlier_half, hits16).astype(BF), ones)
    at = jnp.where(near, jnp.where(rank < 16.0, rank, rank + 16.0), jnp.where(rank < 16.0, rank + 16.0, rank + 24.0))
    row3[...] = jnp.where(hits > 0.5, at, -1.0).reshape(32, 8, 128)
    mask3[...] = mm(mm(any_block, hits16).astype(BF), ones).reshape(32, 8, 128)
    lanes128 = lax.broadcasted_iota(jnp.int32, (256, 128), 1)
    counts = jnp.where(((row[:, 0:128] >> 3) == lanes128) & ((row[:, 0:128] & 7) == 0), mask3[...].reshape(256, 128), 0.0)
    cnt[g] = jnp.broadcast_to(jnp.sum(counts, axis=0, keepdims=True), (8, 128))

    def tell(m, _):
        remote(cnt.at[g], cnt.at[g], s_cnt, r_cnt, plane(m // 4, m % 4)).start()
        return 0

    lax.fori_loop(1, PEERS, tell, 0)

    def forward(b, n, device):
        x_sends.append(remote(block(b), block(b), s_x.at[n], r_x.at[b], device))
        x_sends[-1].start()

    loads[1].wait()
    ship(0, 1, (2, 3, 1, 0))
    ob, oi, oa = xh * 4 + tgt[2], (1 - xh) * 4 + tgt[2], (1 - xh) * 4 + r
    wait(block(ob), r_x.at[ob])
    forward(ob, 3, sib)
    forward(ob, 4, idle)
    wait(block(oi), r_x.at[oi])
    forward(oi, 5, sib)

    place48 = lax.broadcasted_iota(jnp.int32, (ROWS, 128), 0).astype(F32)
    place16 = place48[0:16]
    upper = place16 < 8.0
    place8 = jnp.where(upper, place16, place16 - 8.0)

    def slot_at(m, i):
        dz, dy = m // 4, m % 4
        return (((z + dz) % 4) * 4 + (y + dy) % 4) * 2 + i

    def dispatch(late, part):
        half = (1 - xh) if late else xh
        piece = late * 3 + part

        def pick(m, _):
            for b in range(4):
                here = pl.ds(half * 4 + b, 1)
                if part < 2:
                    chosen = row3[slot_at(m, part), here, :] == place16 + 16.0 * late
                else:
                    both = jnp.where(upper, row3[slot_at(m, 0), here, :], row3[slot_at(m, 1), here, :])
                    chosen = both == place8 + (32.0 + 8.0 * late)
                pmat[pl.ds(pl.multiple_of(m * 16, 16), 16), b * 128 : b * 128 + 128] = jnp.where(chosen, 1.0, 0.0).astype(BF)
            return 0

        lax.fori_loop(0, PEERS, pick, 0)

        def gather(n, _):
            cols = pl.ds(pl.multiple_of(n * 512, 512), 512)
            rows = pl.ds(pl.multiple_of(half * 512, 512), 512)
            send[piece, :, cols] = mm(pmat[0:256, 0:512], xall[rows, cols]).astype(BF)
            return 0

        lax.fori_loop(0, 4, gather, 0)
        slot, base = (part, late * 16) if part < 2 else (late, 32)

        def give(m, _):
            src = send.at[piece, pl.ds(pl.multiple_of(m * 16, 16), 16)]
            dst = recv.at[slot, pl.ds(pl.multiple_of(m * ROWS + base, 16), 16)]
            remote(src, dst, s_d, r_d.at[part % 2], plane(m // 4, m % 4)).start()
            return 0

        lax.fori_loop(1, PEERS, give, 0)
        recv[slot, base : base + 16, :] = send[piece, 0:16, :]

    own_x.wait()
    for b in (xh * 4 + tgt[1], xh * 4 + tgt[3]):
        wait(block(b), r_x.at[b])
    for part in (0, 2, 1):
        dispatch(0, part)
    ship(1, 0, (2, 3, 1, 0))
    wait(block(oa), r_x.at[oa])
    forward(oa, 6, sib)
    ship(1, 1, (2, 3, 1, 0))
    for b in ((1 - xh) * 4 + tgt[1], (1 - xh) * 4 + tgt[3]):
        wait(block(b), r_x.at[b])
    for part in (0, 2, 1):
        dispatch(1, part)
    loads[2].wait()
    order = [(i, k) for k in (1, 0, 2, 3) for i in range(2)]
    for i, k in order:
        choose(i, 2, k)
    for i, k in order:
        post(i, 2, k)

    wait(cnt.at[0:15], r_cnt)

    def before(p, total):
        return total + cnt[p] * jnp.where(p < g, 1.0, 0.0)

    seen = lax.fori_loop(0, PEERS, before, jnp.zeros((8, 128), F32))
    tmp[...] = jnp.transpose(jnp.broadcast_to(seen[0:1, :], (128, 128)))

    def drop(s, _):
        room = find((s // 2) * 2 + xh, 2 * r + s % 2, cap).astype(F32) - tmp[pl.ds(s, 1), :]
        gate3[s] = jnp.where(key3[s] < room, gate3[s], 0.0)
        return 0

    lax.fori_loop(0, 32, drop, 0)

    def weigh(i, half):
        def fill(n, _):
            s = slot_at(half * 8 + n, i)
            at, gate = row3[s], gate3[s]
            for b in range(8):
                spot = (b % 2) * 4 + b // 2
                pmat[pl.ds(pl.multiple_of(n * ROWS, 16), ROWS), spot * 128 : spot * 128 + 128] = jnp.where(
                    at[b : b + 1, :] == place48, gate[b : b + 1, :], 0.0
                ).astype(BF)
            return 0

        lax.fori_loop(0, 8, fill, 0)
        wmat[i, :, half * 384 : half * 384 + 384] = jnp.transpose(pmat[...])

    for i in range(2):
        for half in range(2):
            weigh(i, half)

    width = (xl * 2, xl * 2 + 1, (1 - xl) * 2, (1 - xl) * 2 + 1)

    def block_of(i, w, k):
        return outs[w].at[i, pl.ds(pl.multiple_of(width[k] * 512, 512), 512)]

    def arrived(i, w, k):
        wait(block_of(i, w, k), r_w.at[i, w, width[k]])

    def hidden(i):
        if i == 0:
            wait(recv.at[:, 0:480], r_d.at[0])

            def sort(m, _):
                rows = pl.ds(pl.multiple_of(m * ROWS + 32, 16), 16)
                near, far = recv[0, rows, :].astype(F32), recv[1, rows, :].astype(F32)
                recv[0, rows, :] = jnp.concatenate([near[0:8], far[0:8]], axis=0).astype(BF)
                recv[1, rows, :] = jnp.concatenate([near[8:16], far[8:16]], axis=0).astype(BF)
                return 0

            lax.fori_loop(0, PEERS, sort, 0)
        else:
            wait(recv.at[0, 0:480], r_d.at[1])
        for w in range(2):
            for k in range(4):
                arrived(i, w, k)

        def part(n, _):
            cols = pl.ds(pl.multiple_of(n * 256, 256), 256)
            gate = mm(recv[i], outs[0][i, :, cols])
            up = mm(recv[i], outs[1][i, :, cols])
            hid[i, :, cols] = (gate / (1.0 + jnp.exp(-gate)) * up).astype(BF)
            return 0

        lax.fori_loop(0, 2, part, 0)

    def returned(i, k):
        return big.at[pl.ds((i * 4 + k) * ALL, ALL)]

    def produce(i, k):
        arrived(i, 2, k)
        for n in range(2):
            at = k * 512 + n * 256
            recv[i, :, at : at + 256] = lax.dot_general(
                hid[i], outs[2][i, pl.ds(pl.multiple_of(width[k] * 512 + n * 256, 256), 256), :], (((1,), (1,)), ((), ())), preferred_element_type=F32
            ).astype(BF)

        def give_back(m, _):
            src = recv.at[i, pl.ds(pl.multiple_of(m * ROWS, 16), ROWS), pl.ds(k * 512, 512)]
            dst = big.at[pl.ds(pl.multiple_of((i * 4 + k) * ALL + m * ROWS, 16), ROWS)]
            remote(src, dst, s_ret, r_ret.at[i, k], plane(-(m // 4), -(m % 4))).start()
            return 0

        lax.fori_loop(1, PEERS, give_back, 0)
        big[(i * 4 + k) * ALL : (i * 4 + k) * ALL + ROWS, :] = recv[i, 0:ROWS, k * 512 : k * 512 + 512]

    def partial(k):
        return 6144 + k * 1024

    def sibling(k):
        return 10240 + k * 512

    tail = []

    def combine(k):
        for i in range(2):
            base = (i * 4 + k) * ALL
            wait(big.at[pl.ds(base, 720)], r_ret.at[i, k])
        for n in range(2):
            cols = slice(n * 256, n * 256 + 256)
            total = mm(wmat[0], big[k * ALL : k * ALL + ALL, cols])
            total = total + mm(wmat[1], big[(4 + k) * ALL : (4 + k) * ALL + ALL, cols])
            big[partial(k) : partial(k) + 1024, cols] = total.astype(BF)
        k2 = k
        tail.append(
            remote(
                big.at[pl.ds(pl.multiple_of(partial(k) + (1 - c) * 512, 512), 512)],
                big.at[pl.ds(sibling(k2), 512)],
                s_sib.at[k], r_sib.at[k2], sib,
            )
        )
        tail[-1].start()

    def own(k):
        return pl.multiple_of(partial(k) + c * 512, 512)

    def to_idle(k):
        wait(big.at[pl.ds(sibling(k), 512)], r_sib.at[k])
        both = big[pl.ds(own(k), 512), :].astype(F32) + big[sibling(k) : sibling(k) + 512, :].astype(F32)
        big[pl.ds(own(k), 512), :] = both.astype(BF)
        k2 = k ^ 2
        tail.append(
            remote(
                big.at[pl.ds(pl.multiple_of(own(k) + (1 - xh) * 256, 256), 256)],
                idr.at[k2], s_idle.at[k], r_idle.at[k2], idle,
            )
        )
        tail[-1].start()

    def to_busy(k):
        wait(idr.at[k], r_idle.at[k])
        there = pl.multiple_of((1 - xl) * 128, 128)
        mine = big[pl.ds(pl.multiple_of(own(k) + xh * 256 + (1 - xl) * 128, 128), 128), :].astype(F32)
        bout[k] = (mine + idr[k, pl.ds(there, 128), :].astype(F32)).astype(BF)
        k2 = k ^ 2
        tail.append(remote(bout.at[k], binr.at[k2], s_busy.at[k], r_busy.at[k2], busy))
        tail[-1].start()

    def finish(k):
        wait(binr.at[k], r_busy.at[k])
        here = pl.multiple_of(xl * 128, 128)
        mine = big[pl.ds(pl.multiple_of(own(k) + xh * 256 + xl * 128, 128), 128), :].astype(F32)
        total = mine + idr[k, pl.ds(here, 128), :].astype(F32) + binr[k].astype(F32)
        comb[:, pl.ds(pl.multiple_of(width[k] * 512, 512), 512)] = total.astype(BF)

    hidden(0)
    produce(0, 0)
    produce(0, 1)
    hidden(1)
    produce(1, 0)
    produce(1, 1)

    def late_blocks():
        for k in (2, 3):
            for i in range(2):
                produce(i, k)

    @pl.when(c == 0)
    def _():
        late_blocks()

    combine(0)
    combine(1)
    to_idle(0)
    to_idle(1)

    @pl.when(c == 1)
    def _():
        late_blocks()

    combine(2)
    to_idle(2)
    to_busy(2)
    combine(3)
    to_idle(3)
    to_busy(3)
    to_busy(0)
    to_busy(1)
    for k in range(4):
        finish(k)

    for copy in x_sends + tail:
        copy.wait_send()
    wait(meta.at[0:7], s_meta)
    wait(stage.at[0:18], s_w)
    wait(cnt.at[0:15], s_cnt)
    wait(recv.at[:, 0:720], s_d)
    wait(recv.at[:, 0:720], s_ret)


def local(tokens, expert_ids, router_scores, lane_list, capacity, train_gate, train_up, train_down):
    dma = pltpu.SemaphoreType.DMA
    out_w = pltpu.VMEM((2, D, H), BF)
    anywhere = pl.BlockSpec(memory_space=pl.ANY)
    vmem = pl.BlockSpec(memory_space=pltpu.VMEM)
    smem = pl.BlockSpec(memory_space=pltpu.SMEM)
    return pl.pallas_call(
        kernel,
        out_shape=(jax.ShapeDtypeStruct((128, D), BF), out_w, out_w, out_w),
        in_specs=[anywhere, vmem, vmem, smem, smem, anywhere, anywhere, anywhere],
        out_specs=[vmem, vmem, vmem, vmem],
        scratch_shapes=[
            pltpu.VMEM((12288, 512), BF),
            pltpu.VMEM((24, 512, 512), BF),
            pltpu.VMEM((1024, D), BF),
            pltpu.VMEM((6, 256, D), BF),
            pltpu.VMEM((2, ALL, D), BF),
            pltpu.VMEM((384, 1024), BF),
            pltpu.VMEM((2, 1024, ALL), BF),
            pltpu.VMEM((2, ALL, H), BF),
            pltpu.VMEM((4, 256, 512), BF),
            pltpu.VMEM((4, 128, 512), BF),
            pltpu.VMEM((4, 128, 512), BF),
            pltpu.VMEM((8, 32, 128), F32),
            pltpu.VMEM((32, 8, 128), F32),
            pltpu.VMEM((32, 8, 128), F32),
            pltpu.VMEM((32, 8, 128), F32),
            pltpu.VMEM((32, 8, 128), F32),
            pltpu.VMEM((16, 8, 128), F32),
            pltpu.VMEM((128, 128), F32),
            dma((3,)), dma((7,)), dma((8,)), dma, dma, dma, dma((2, 3, 4)), dma, dma,
            dma, dma((2,)), dma, dma((2, 4)),
            dma((4,)), dma((4,)), dma((4,)), dma((4,)), dma((4,)), dma((4,)), dma,
        ],
        compiler_params=pltpu.CompilerParams(
            collective_id=0, has_side_effects=True, vmem_limit_bytes=50 << 20
        ),
        name="resync_moe",
    )(
        tokens, expert_ids.T, router_scores.T, lane_list, capacity,
        train_gate.reshape(4096, 512), train_up.reshape(4096, 512), train_down.reshape(4096, 512),
    )


def solution(mesh):
    both = ("expert", "replica")
    return jax.shard_map(
        local,
        mesh=mesh,
        in_specs=(
            P(both, None), P(both, None), P(both, None), P(), P(),
            P("expert", "replica", None), P("expert", "replica", None), P("expert", "replica", None),
        ),
        out_specs=(P(both, None), P(both, None, None), P(both, None, None), P(both, None, None)),
        check_vma=False,
    )
```

```python
import jax
import jax.numpy as jnp
from jax import lax
from jax.experimental import pallas as pl
from jax.experimental.pallas import tpu as pltpu
from jax.sharding import PartitionSpec as P

MESH = pl.DeviceIdType.MESH
BF = jnp.bfloat16
F32 = jnp.float32
ROWS = 48
PEERS = 16
ALL = ROWS * PEERS
D = 2048
H = 512


def kernel(
    tok, ids, scores, lane, cap, tg, tu, td,
    comb, og, ou, od,
    big, stage, xall, send, recv, pmat, wmat, hid, idr, bout, binr,
    meta, mask3, key3, row3, gate3, cnt, tmp,
    s_t, s_x, r_x, s_meta, r_meta, s_w, r_w, s_cnt, r_cnt, s_d, r_d,
    s_ret, r_ret, s_sib, r_sib, s_idle, r_idle, s_busy, r_busy, l_x,
):
    e = lax.axis_index("expert")
    r = lax.axis_index("replica")
    g, xh = e // 2, e % 2
    xl, c = r // 2, r % 2
    z, y = g // 4, g % 4
    o = xh * 4 + r
    tgt = (r, r + 1 - 2 * c, (r + 2) % 4, 3 - r)
    e_far = e + 1 - 2 * xh
    train, outs = (tg, tu, td), (og, ou, od)

    def dev(ee, rr):
        return {"expert": ee, "replica": rr}

    def plane(dz, dy):
        return dev((((z + dz + 4) % 4) * 4 + (y + dy + 4) % 4) * 2 + xh, r)

    def remote(src, dst, ssem, rsem, device):
        return pltpu.make_async_remote_copy(
            src_ref=src, dst_ref=dst, send_sem=ssem, recv_sem=rsem, device_id=device, device_id_type=MESH
        )

    def wait(ref, sem):
        pltpu.make_async_copy(ref, ref, sem).wait()

    loads = [pltpu.make_async_copy(train[w], big.at[pl.ds(w * 4096, 4096)], s_t.at[w]) for w in range(3)]
    for copy in loads:
        copy.start()
    meta[o, 0:10, :] = ids[...].astype(F32)
    raw = scores[...]
    grown = jnp.exp(raw - jnp.max(raw, axis=0, keepdims=True))
    meta[o, 16:26, :] = grown / jnp.sum(grown, axis=0, keepdims=True)

    lanes = [lane[e * 8 + j] for j in range(8)]
    tgts = (r, r + 1 - 2 * c, (1 - xl) * 2, (1 - xl) * 2 + 1)

    def choose(i, w, k):
        n = (i * 3 + w) * 4 + k

        def some(t, _):
            at = pl.multiple_of(t * 64, 64)
            kept = big[pl.ds(pl.multiple_of(w * 4096 + at, 64), 64), :]
            for j in range(1, 8):
                other = big[pl.ds(pl.multiple_of((w * 8 + j) * 512 + at, 64), 64), :]
                kept = lax.select(lanes[j] == 2 * tgts[k] + i, other, kept)
            stage[n, pl.ds(at, 64), :] = kept
            return 0

        lax.fori_loop(0, 8, some, 0)

    def post(i, w, k):
        n = (i * 3 + w) * 4 + k
        place = outs[w].at[i, pl.ds(pl.multiple_of(r * 512, 512), 512)]
        if k:
            remote(stage.at[n], place, s_w, r_w.at[i, w, r], dev(e, tgts[k])).start()
        else:
            pltpu.make_async_copy(stage.at[n], place, r_w.at[i, w, r]).start()

    def ship(i, w, ks):
        for k in ks:
            choose(i, w, k)
            post(i, w, k)

    barrier = pltpu.get_barrier_semaphore()
    group = [dev(e if f < 4 else e_far, tgt[f % 4]) for f in range(1, 8)]
    for device in group:
        pl.semaphore_signal(barrier, inc=1, device_id=device, device_id_type=MESH)

    def greet(m, _):
        pl.semaphore_signal(barrier, inc=1, device_id=plane(m // 4, m % 4), device_id_type=MESH)
        return 0

    lax.fori_loop(1, PEERS, greet, 0)
    loads[0].wait()
    for k in (2, 3, 1, 0):
        choose(0, 0, k)
    pl.semaphore_wait(barrier, 7 + PEERS - 1)

    def block(b):
        return xall.at[pl.ds(pl.multiple_of(b * 128, 128), 128)]

    sib, busy, idle = dev(e, tgt[1]), dev(e, tgt[2]), dev(e_far, tgt[2])
    x_sends = [
        remote(tok, block(o), s_x.at[0], r_x.at[o], busy),
        remote(tok, block(o), s_x.at[1], r_x.at[o], idle),
        remote(tok, block(o), s_x.at[2], r_x.at[o], sib),
    ]
    for copy in x_sends:
        copy.start()
    own_x = pltpu.make_async_copy(tok, block(o), l_x)
    own_x.start()
    for device in group:
        remote(meta.at[o], meta.at[o], s_meta, r_meta, device).start()
    for k in (2, 3, 1, 0):
        post(0, 0, k)

    wait(meta.at[0:7], r_meta)
    named = [meta[:, k, :] for k in range(10)]
    gates = [meta[:, 16 + k, :] for k in range(10)]

    def find(column, k, table=None):
        at = jnp.int32(0)
        for j in range(8):
            at = at + jnp.where(lane[column * 8 + j] == k, j if table is None else table[column * 8 + j], 0)
        return at

    def expert_of(s):
        column = (s // 2) * 2 + xh
        return column * 8 + find(column, 2 * r + s % 2)

    def one_slot(s, _):
        expert = expert_of(s).astype(F32)
        hits = jnp.zeros((8, 128), F32)
        gate = jnp.zeros((8, 128), F32)
        for k in range(10):
            same = named[k] == expert
            hits = hits + jnp.where(same, 1.0, 0.0)
            gate = gate + jnp.where(same, gates[k], 0.0)
        mask3[s] = hits
        gate3[s] = gate
        return 0

    lax.fori_loop(0, 32, one_slot, 0)
    hits = mask3[...].reshape(256, 128)
    hits16 = hits.astype(BF)
    row = lax.broadcasted_iota(jnp.int32, (256, 256), 0)
    col = lax.broadcasted_iota(jnp.int32, (256, 256), 1)
    slot_same = (row >> 3) == (col >> 3)
    earlier_block = jnp.where(slot_same & (col < row), 1.0, 0.0).astype(BF)
    earlier_half = jnp.where(((row >> 2) == (col >> 2)) & (col < row), 1.0, 0.0).astype(BF)
    any_block = jnp.where(slot_same, 1.0, 0.0).astype(BF)
    earlier_token = jnp.where(row[0:128, 0:128] < col[0:128, 0:128], 1.0, 0.0).astype(BF)
    ones = jnp.ones((128, 128), BF)

    def mm(a, b):
        return jnp.dot(a, b, preferred_element_type=F32)

    within = mm(hits16, earlier_token)
    rank = within + mm(mm(earlier_block, hits16).astype(BF), ones)
    key3[...] = rank.reshape(32, 8, 128)
    near = ((row[:, 0:128] >> 2) % 2) == xh
    rank = within + mm(mm(earlier_half, hits16).astype(BF), ones)
    at = jnp.where(near, jnp.where(rank < 16.0, rank, rank + 16.0), jnp.where(rank < 16.0, rank + 16.0, rank + 24.0))
    row3[...] = jnp.where(hits > 0.5, at, -1.0).reshape(32, 8, 128)
    mask3[...] = mm(mm(any_block, hits16).astype(BF), ones).reshape(32, 8, 128)
    lanes128 = lax.broadcasted_iota(jnp.int32, (256, 128), 1)
    counts = jnp.where(((row[:, 0:128] >> 3) == lanes128) & ((row[:, 0:128] & 7) == 0), mask3[...].reshape(256, 128), 0.0)
    cnt[g] = jnp.broadcast_to(jnp.sum(counts, axis=0, keepdims=True), (8, 128))

    def tell(m, _):
        remote(cnt.at[g], cnt.at[g], s_cnt, r_cnt, plane(m // 4, m % 4)).start()
        return 0

    lax.fori_loop(1, PEERS, tell, 0)

    def forward(b, n, device):
        x_sends.append(remote(block(b), block(b), s_x.at[n], r_x.at[b], device))
        x_sends[-1].start()

    loads[1].wait()
    ship(0, 1, (2, 3, 1, 0))
    ob, oi, oa = xh * 4 + tgt[2], (1 - xh) * 4 + tgt[2], (1 - xh) * 4 + r
    wait(block(ob), r_x.at[ob])
    forward(ob, 3, sib)
    forward(ob, 4, idle)
    wait(block(oi), r_x.at[oi])
    forward(oi, 5, sib)

    place48 = lax.broadcasted_iota(jnp.int32, (ROWS, 128), 0).astype(F32)
    place16 = place48[0:16]
    upper = place16 < 8.0
    place8 = jnp.where(upper, place16, place16 - 8.0)

    def slot_at(m, i):
        dz, dy = m // 4, m % 4
        return (((z + dz) % 4) * 4 + (y + dy) % 4) * 2 + i

    def dispatch(late, part):
        half = (1 - xh) if late else xh
        piece = late * 3 + part

        def pick(m, _):
            for b in range(4):
                here = pl.ds(half * 4 + b, 1)
                if part < 2:
                    chosen = row3[slot_at(m, part), here, :] == place16 + 16.0 * late
                else:
                    both = jnp.where(upper, row3[slot_at(m, 0), here, :], row3[slot_at(m, 1), here, :])
                    chosen = both == place8 + (32.0 + 8.0 * late)
                pmat[pl.ds(pl.multiple_of(m * 16, 16), 16), b * 128 : b * 128 + 128] = jnp.where(chosen, 1.0, 0.0).astype(BF)
            return 0

        lax.fori_loop(0, PEERS, pick, 0)

        def gather(n, _):
            cols = pl.ds(pl.multiple_of(n * 512, 512), 512)
            rows = pl.ds(pl.multiple_of(half * 512, 512), 512)
            send[piece, :, cols] = mm(pmat[0:256, 0:512], xall[rows, cols]).astype(BF)
            return 0

        lax.fori_loop(0, 4, gather, 0)
        slot, base = (part, late * 16) if part < 2 else (late, 32)

        def give(m, _):
            src = send.at[piece, pl.ds(pl.multiple_of(m * 16, 16), 16)]
            dst = recv.at[slot, pl.ds(pl.multiple_of(m * ROWS + base, 16), 16)]
            remote(src, dst, s_d, r_d.at[part % 2], plane(m // 4, m % 4)).start()
            return 0

        lax.fori_loop(1, PEERS, give, 0)
        recv[slot, base : base + 16, :] = send[piece, 0:16, :]

    own_x.wait()
    for b in (xh * 4 + tgt[1], xh * 4 + tgt[3]):
        wait(block(b), r_x.at[b])
    for part in (0, 2, 1):
        dispatch(0, part)
    ship(1, 0, (2, 3, 1, 0))
    wait(block(oa), r_x.at[oa])
    forward(oa, 6, sib)
    ship(1, 1, (2, 3, 1, 0))
    for b in ((1 - xh) * 4 + tgt[1], (1 - xh) * 4 + tgt[3]):
        wait(block(b), r_x.at[b])
    for part in (0, 2, 1):
        dispatch(1, part)
    loads[2].wait()
    order = [(i, k) for k in (1, 0, 2, 3) for i in range(2)]
    for i, k in order:
        choose(i, 2, k)
    for i, k in order:
        post(i, 2, k)

    wait(cnt.at[0:15], r_cnt)

    def before(p, total):
        return total + cnt[p] * jnp.where(p < g, 1.0, 0.0)

    seen = lax.fori_loop(0, PEERS, before, jnp.zeros((8, 128), F32))
    tmp[...] = jnp.transpose(jnp.broadcast_to(seen[0:1, :], (128, 128)))

    def drop(s, _):
        room = find((s // 2) * 2 + xh, 2 * r + s % 2, cap).astype(F32) - tmp[pl.ds(s, 1), :]
        gate3[s] = jnp.where(key3[s] < room, gate3[s], 0.0)
        return 0

    lax.fori_loop(0, 32, drop, 0)

    def weigh(i, half):
        def fill(n, _):
            s = slot_at(half * 8 + n, i)
            at, gate = row3[s], gate3[s]
            for b in range(8):
                spot = (b % 2) * 4 + b // 2
                pmat[pl.ds(pl.multiple_of(n * ROWS, 16), ROWS), spot * 128 : spot * 128 + 128] = jnp.where(
                    at[b : b + 1, :] == place48, gate[b : b + 1, :], 0.0
                ).astype(BF)
            return 0

        lax.fori_loop(0, 8, fill, 0)
        wmat[i, :, half * 384 : half * 384 + 384] = jnp.transpose(pmat[...])

    for i in range(2):
        for half in range(2):
            weigh(i, half)

    width = (xl * 2, xl * 2 + 1, (1 - xl) * 2, (1 - xl) * 2 + 1)

    def block_of(i, w, k):
        return outs[w].at[i, pl.ds(pl.multiple_of(width[k] * 512, 512), 512)]

    def arrived(i, w, k):
        wait(block_of(i, w, k), r_w.at[i, w, width[k]])

    def hidden(i):
        if i == 0:
            wait(recv.at[:, 0:480], r_d.at[0])

            def sort(m, _):
                rows = pl.ds(pl.multiple_of(m * ROWS + 32, 16), 16)
                near, far = recv[0, rows, :].astype(F32), recv[1, rows, :].astype(F32)
                recv[0, rows, :] = jnp.concatenate([near[0:8], far[0:8]], axis=0).astype(BF)
                recv[1, rows, :] = jnp.concatenate([near[8:16], far[8:16]], axis=0).astype(BF)
                return 0

            lax.fori_loop(0, PEERS, sort, 0)
        else:
            wait(recv.at[0, 0:480], r_d.at[1])
        for w in range(2):
            for k in range(4):
                arrived(i, w, k)

        def part(n, _):
            cols = pl.ds(pl.multiple_of(n * 256, 256), 256)
            gate = mm(recv[i], outs[0][i, :, cols])
            up = mm(recv[i], outs[1][i, :, cols])
            hid[i, :, cols] = (gate / (1.0 + jnp.exp(-gate)) * up).astype(BF)
            return 0

        lax.fori_loop(0, 2, part, 0)

    def returned(i, k):
        return big.at[pl.ds((i * 4 + k) * ALL, ALL)]

    def produce(i, k):
        arrived(i, 2, k)
        for n in range(2):
            at = k * 512 + n * 256
            recv[i, :, at : at + 256] = lax.dot_general(
                hid[i], outs[2][i, pl.ds(pl.multiple_of(width[k] * 512 + n * 256, 256), 256), :], (((1,), (1,)), ((), ())), preferred_element_type=F32
            ).astype(BF)

        def give_back(m, _):
            src = recv.at[i, pl.ds(pl.multiple_of(m * ROWS, 16), ROWS), pl.ds(k * 512, 512)]
            dst = big.at[pl.ds(pl.multiple_of((i * 4 + k) * ALL + m * ROWS, 16), ROWS)]
            remote(src, dst, s_ret, r_ret.at[i, k], plane(-(m // 4), -(m % 4))).start()
            return 0

        lax.fori_loop(1, PEERS, give_back, 0)
        big[(i * 4 + k) * ALL : (i * 4 + k) * ALL + ROWS, :] = recv[i, 0:ROWS, k * 512 : k * 512 + 512]

    def partial(k):
        return 6144 + k * 1024

    def sibling(k):
        return 10240 + k * 512

    tail = []

    def combine(k):
        for i in range(2):
            base = (i * 4 + k) * ALL
            wait(big.at[pl.ds(base, 720)], r_ret.at[i, k])

        def sums(core):
            rows = pl.ds(pl.multiple_of(core * 512, 512), 512)
            for n in range(2):
                cols = slice(n * 256, n * 256 + 256)
                total = mm(wmat[0, rows, :], big[k * ALL : k * ALL + ALL, cols])
                total = total + mm(wmat[1, rows, :], big[(4 + k) * ALL : (4 + k) * ALL + ALL, cols])
                big[pl.ds(pl.multiple_of(partial(k) + core * 512, 512), 512), cols] = total.astype(BF)

        sums(1 - c)
        tail.append(
            remote(
                big.at[pl.ds(pl.multiple_of(partial(k) + (1 - c) * 512, 512), 512)],
                big.at[pl.ds(sibling(k), 512)],
                s_sib.at[k], r_sib.at[k], sib,
            )
        )
        tail[-1].start()
        sums(c)

    def own(k):
        return pl.multiple_of(partial(k) + c * 512, 512)

    def to_idle(k):
        wait(big.at[pl.ds(sibling(k), 512)], r_sib.at[k])
        both = big[pl.ds(own(k), 512), :].astype(F32) + big[sibling(k) : sibling(k) + 512, :].astype(F32)
        big[pl.ds(own(k), 512), :] = both.astype(BF)
        k2 = k ^ 2
        for n, part in enumerate((xl, 1 - xl)):
            tail.append(
                remote(
                    big.at[pl.ds(pl.multiple_of(own(k) + (1 - xh) * 256 + part * 128, 128), 128)],
                    idr.at[k2, pl.ds(pl.multiple_of(part * 128, 128), 128)],
                    s_idle.at[k, n], r_idle.at[k2, n], idle,
                )
            )
            tail[-1].start()

    def to_busy(k):
        there = pl.multiple_of((1 - xl) * 128, 128)
        wait(idr.at[k, pl.ds(there, 128)], r_idle.at[k, 0])
        mine = big[pl.ds(pl.multiple_of(own(k) + xh * 256 + (1 - xl) * 128, 128), 128), :].astype(F32)
        bout[k] = (mine + idr[k, pl.ds(there, 128), :].astype(F32)).astype(BF)
        k2 = k ^ 2
        tail.append(remote(bout.at[k], binr.at[k2], s_busy.at[k], r_busy.at[k2], busy))
        tail[-1].start()

    def finish(k):
        here = pl.multiple_of(xl * 128, 128)
        wait(idr.at[k, pl.ds(here, 128)], r_idle.at[k, 1])
        wait(binr.at[k], r_busy.at[k])
        mine = big[pl.ds(pl.multiple_of(own(k) + xh * 256 + xl * 128, 128), 128), :].astype(F32)
        total = mine + idr[k, pl.ds(here, 128), :].astype(F32) + binr[k].astype(F32)
        comb[:, pl.ds(pl.multiple_of(width[k] * 512, 512), 512)] = total.astype(BF)

    hidden(0)
    produce(0, 0)
    produce(0, 1)
    hidden(1)
    produce(1, 0)
    produce(1, 1)

    def late_blocks():
        for k in (2, 3):
            for i in range(2):
                produce(i, k)

    @pl.when(c == 0)
    def _():
        late_blocks()

    combine(0)
    combine(1)
    to_idle(0)
    to_idle(1)

    @pl.when(c == 1)
    def _():
        late_blocks()

    combine(2)
    to_idle(2)
    to_busy(2)
    combine(3)
    to_idle(3)
    to_busy(3)
    to_busy(0)
    to_busy(1)
    for k in range(4):
        finish(k)

    for copy in x_sends + tail:
        copy.wait_send()
    wait(meta.at[0:7], s_meta)
    wait(stage.at[0:18], s_w)
    wait(cnt.at[0:15], s_cnt)
    wait(recv.at[:, 0:720], s_d)
    wait(recv.at[:, 0:720], s_ret)


def local(tokens, expert_ids, router_scores, lane_list, capacity, train_gate, train_up, train_down):
    dma = pltpu.SemaphoreType.DMA
    out_w = pltpu.VMEM((2, D, H), BF)
    anywhere = pl.BlockSpec(memory_space=pl.ANY)
    vmem = pl.BlockSpec(memory_space=pltpu.VMEM)
    smem = pl.BlockSpec(memory_space=pltpu.SMEM)
    return pl.pallas_call(
        kernel,
        out_shape=(jax.ShapeDtypeStruct((128, D), BF), out_w, out_w, out_w),
        in_specs=[anywhere, vmem, vmem, smem, smem, anywhere, anywhere, anywhere],
        out_specs=[vmem, vmem, vmem, vmem],
        scratch_shapes=[
            pltpu.VMEM((12288, 512), BF),
            pltpu.VMEM((24, 512, 512), BF),
            pltpu.VMEM((1024, D), BF),
            pltpu.VMEM((6, 256, D), BF),
            pltpu.VMEM((2, ALL, D), BF),
            pltpu.VMEM((384, 1024), BF),
            pltpu.VMEM((2, 1024, ALL), BF),
            pltpu.VMEM((2, ALL, H), BF),
            pltpu.VMEM((4, 256, 512), BF),
            pltpu.VMEM((4, 128, 512), BF),
            pltpu.VMEM((4, 128, 512), BF),
            pltpu.VMEM((8, 32, 128), F32),
            pltpu.VMEM((32, 8, 128), F32),
            pltpu.VMEM((32, 8, 128), F32),
            pltpu.VMEM((32, 8, 128), F32),
            pltpu.VMEM((32, 8, 128), F32),
            pltpu.VMEM((16, 8, 128), F32),
            pltpu.VMEM((128, 128), F32),
            dma((3,)), dma((7,)), dma((8,)), dma, dma, dma, dma((2, 3, 4)), dma, dma,
            dma, dma((2,)), dma, dma((2, 4)),
            dma((4,)), dma((4,)), dma((4, 2)), dma((4, 2)), dma((4,)), dma((4,)), dma,
        ],
        compiler_params=pltpu.CompilerParams(
            collective_id=0, has_side_effects=True, vmem_limit_bytes=50 << 20
        ),
        name="resync_moe",
    )(
        tokens, expert_ids.T, router_scores.T, lane_list, capacity,
        train_gate.reshape(4096, 512), train_up.reshape(4096, 512), train_down.reshape(4096, 512),
    )


def solution(mesh):
    both = ("expert", "replica")
    return jax.shard_map(
        local,
        mesh=mesh,
        in_specs=(
            P(both, None), P(both, None), P(both, None), P(), P(),
            P("expert", "replica", None), P("expert", "replica", None), P("expert", "replica", None),
        ),
        out_specs=(P(both, None), P(both, None, None), P(both, None, None), P(both, None, None)),
        check_vma=False,
    )
```
